128 devices in a mesh: block: 16 (over z_hi, x, core), line: 8 (over z_lo, y).
Axes of the slice: x: 4, y: 4, z: 4 (z_hi: 2, z_lo: 2; z = z_hi * 2 + z_lo), core: 2. Of those that a mesh axis runs over, the one named last changes fastest.
Arguments:
- adjoint_start: float32 [6, 16, 128, 1024], P(None, 'block', 'line'), may hold values from -6 to 6
- source: float32 [6, 16, 128, 1024], P(None, 'block', 'line'), may hold values from -6 to 6
- jacobian: float32 [6, 6, 16, 128, 1024], P(None, None, 'block', 'line'), may hold values from -0.45 to 3.6
- inv_diag: float32 [6, 6, 16, 128, 1024], P(None, None, 'block', 'line'), may hold values from -1 to 1
- lower_prop: float32 [6, 6, 16, 128, 1024], P(None, None, 'block', 'line'), may hold values from -1 to 1, as said below
- upper_prop: float32 [6, 6, 16, 128, 1024], P(None, None, 'block', 'line'), may hold values from -1 to 1, as said below
- send_cells: int32 [16, 8, 16, 512], P('block', 'line'), may hold values from -1 to 16383, as said below
- recv_cells: int32 [16, 8, 16, 512], P('block', 'line'), may hold values from -1 to 16383, as said below
- face_weight: float32 [16, 8, 16, 512], P('block', 'line'), may hold values from 0.2 to 0.6
- cycle_cells: int32 [16, 8, 512], P('block', 'line'), may hold values from 0 to 16383
- iface_cells: int32 [16, 8, 512], P('block', 'line'), may hold values from -1 to 16383, as said below
- iface_donor: int32 [16, 8, 2, 512], P('block', 'line'), may hold values from 0 to 8191, as said below
- iface_weight: float32 [16, 8, 2, 512], P('block', 'line'), may hold values from 0.1 to 0.5
Outputs:
- adjoint: float32 [6, 16, 128, 1024], P(None, 'block', 'line')
The draws below stay inside these ranges and needn't reach their ends.
Inputs may be any that keep to these rules, and one draw needn't show every extreme that they name: For every source block p, destination block b and line group q, slot s of send_cells[p, q, b] is live (not -1) exactly when slot s of recv_cells[b, q, p] is; live slots come first; a block never faces itself, and every block receives 512 live slots from the next block (index b + 1 modulo 16). `recv_cells`: same liveness as send_cells; several slots may feed one cell. `iface_cells`: live slots come first; the devices of block 0 have all 512 slots live. `iface_donor`: the second donor of a slot is the first plus one. `lower_prop`: lower triangular in the variables. `upper_prop`: upper triangular in the variables.
All inputs are finite; a program needn't handle non-finite values.
Results may differ from the reference program's by a relative error of at most 0.0001.
Values sent between devices are 32-bit elements; how exact they have to be, the bound alone decides.
No kernel may reach another device: no remote copies, remote signals or barrier semaphores. Data moves between devices by JAX's collectives and lax.ppermute only.
A program may use at most 384 MiB of HBM per device.

```python
import math
from functools import partial
import jax
import jax.numpy as jnp
from jax import lax

NVAR = 6
WALL_LINES = 1024
SLOTS = 512
CYCLE = 512
IFACE = 512
ITERS = 2
GRID_BLOCKS = 16
GROUPS = 8
NORMAL_CELLS = 128
CELLS = 16384


def decay_rates(key, slow_share):
    subkey = jax.random.fold_in(key, 901)
    choose_key, spread_key = jax.random.split(subkey)
    slow = jax.random.uniform(choose_key, (6, GRID_BLOCKS, 1, 1)) < slow_share
    spread = jax.random.uniform(spread_key, (6, GRID_BLOCKS, 1, WALL_LINES), minval=0.3, maxval=1.0)
    slow_rate = jnp.exp(-math.log(10.0) / NORMAL_CELLS * spread)
    fast_rate = jnp.exp(-1.0 / (30.0 + 20.0 * spread))
    return jnp.where(slow, slow_rate, fast_rate)


def face_counts(key):
    subkey = jax.random.fold_in(key, 501)
    shape = (GRID_BLOCKS, GROUPS, GRID_BLOCKS)
    counts = jax.random.randint(subkey, shape, SLOTS // 4, SLOTS + 1)
    dest_index = lax.broadcasted_iota(jnp.int32, shape, 0)
    source_index = lax.broadcasted_iota(jnp.int32, shape, 2)
    counts = jnp.where(source_index == (dest_index + 1) % GRID_BLOCKS, SLOTS, counts)
    return jnp.where(source_index == dest_index, 0, counts)


def identity_mask():
    rows = lax.broadcasted_iota(jnp.int32, (6, 6, 1, 1, 1), 0)
    columns = lax.broadcasted_iota(jnp.int32, (6, 6, 1, 1, 1), 1)
    return (rows, columns)


def slow_share_value():
    share = 0.5
    return share


def propagator(key, decay_speeds, lower_side):
    jump_random_key, factor_random_key, perturbation_key = jax.random.split(key, 3)
    sudden_jump = jax.random.bernoulli(jump_random_key, 3.0 / NORMAL_CELLS, (1, GRID_BLOCKS, NORMAL_CELLS, WALL_LINES))
    scale_factor = jax.random.uniform(factor_random_key, (1, GRID_BLOCKS, NORMAL_CELLS, WALL_LINES), minval=0.5, maxval=0.8)
    diagonal_block = decay_speeds * jnp.where(sudden_jump, scale_factor, 1.0)
    scale = jnp.sqrt((1.0 - decay_speeds)[:, None] * (1.0 - decay_speeds)[None, :])
    noise = jax.random.uniform(perturbation_key, (6, 6, GRID_BLOCKS, NORMAL_CELLS, WALL_LINES), minval=-1.0, maxval=1.0)
    rows, columns = identity_mask()
    if lower_side:
        keep = rows > columns
    else:
        keep = rows < columns
    matrix = jnp.where(keep, 0.3 * scale * noise, 0.0)
    return jnp.where(rows == columns, diagonal_block[None], matrix)


def draw_jacobian(key, part):
    key = jax.random.fold_in(key, 1)
    diag_key, off_key = jax.random.split(key)
    shape = (6, 6, GRID_BLOCKS, NORMAL_CELLS, WALL_LINES)
    diagonal_block = jax.random.uniform(diag_key, shape, minval=1.5, maxval=3.0)
    off = jax.random.uniform(off_key, shape, minval=-0.35, maxval=0.35)
    rows, columns = identity_mask()
    return jnp.where(rows == columns, diagonal_block, off)


def draw_inv_diag(key, part):
    decay_speeds = decay_rates(key, slow_share_value())
    key = jax.random.fold_in(key, 2)
    gain_key, perturbation_key = jax.random.split(key)
    gain = jax.random.uniform(gain_key, (6, GRID_BLOCKS, NORMAL_CELLS, WALL_LINES), minval=0.25, maxval=0.5)
    diagonal_block = gain * (1.0 - decay_speeds) * (1.0 - decay_speeds)
    noise = jax.random.uniform(perturbation_key, (6, 6, GRID_BLOCKS, NORMAL_CELLS, WALL_LINES), minval=-1.0, maxval=1.0)
    off = 0.25 * jnp.sqrt(diagonal_block[:, None] * diagonal_block[None, :]) * noise
    rows, columns = identity_mask()
    return jnp.where(rows == columns, diagonal_block[None], off)


def draw_lower_prop(key, part):
    decay_speeds = decay_rates(key, slow_share_value())
    key = jax.random.fold_in(key, 3)
    return propagator(key, decay_speeds, True)


def draw_upper_prop(key, part):
    decay_speeds = decay_rates(key, slow_share_value())
    key = jax.random.fold_in(key, 4)
    return propagator(key, decay_speeds, False)


def draw_send_cells(key, part):
    counts = face_counts(key)
    key = jax.random.fold_in(key, 5)
    shape = (GRID_BLOCKS, GROUPS, GRID_BLOCKS, SLOTS)
    chosen = jax.random.randint(key, shape, 0, CELLS)
    chosen = chosen.at[1, 0, 0, 0].set(CELLS - 1)
    live_count = jnp.transpose(counts, (2, 1, 0))
    slot_index = lax.broadcasted_iota(jnp.int32, shape, 3)
    return jnp.where(slot_index < live_count[..., None], chosen, -1)


def draw_recv_cells(key, part):
    counts = face_counts(key)
    key = jax.random.fold_in(key, 6)
    shape = (GRID_BLOCKS, GROUPS, GRID_BLOCKS, SLOTS)
    chosen = jax.random.randint(key, shape, 0, CELLS)
    chosen = chosen.at[0, 0, 1, 0].set(CELLS - 1)
    slot_index = lax.broadcasted_iota(jnp.int32, shape, 3)
    return jnp.where(slot_index < counts[..., None], chosen, -1)


def draw_cycle_cells(key, part):
    key = jax.random.fold_in(key, 7)
    chosen = jax.random.randint(key, (GRID_BLOCKS, GROUPS, CYCLE), 0, CELLS)
    return chosen.at[0, 0, 0].set(CELLS - 1)


def draw_iface_cells(key, part):
    key = jax.random.fold_in(key, 8)
    count_key, cell_key = jax.random.split(key)
    counts = jax.random.randint(count_key, (GRID_BLOCKS, GROUPS, 1), IFACE // 2, IFACE + 1)
    block_index = lax.broadcasted_iota(jnp.int32, (GRID_BLOCKS, GROUPS, 1), 0)
    counts = jnp.where(block_index == 0, IFACE, counts)
    chosen = jax.random.randint(cell_key, (GRID_BLOCKS, GROUPS, IFACE), 0, CELLS)
    chosen = chosen.at[0, 0, 0].set(CELLS - 1)
    slot_index = lax.broadcasted_iota(jnp.int32, (GRID_BLOCKS, GROUPS, IFACE), 2)
    return jnp.where(slot_index < counts, chosen, -1)


def draw_iface_donor(key, part):
    key = jax.random.fold_in(key, 9)
    first = jax.random.randint(key, (GRID_BLOCKS, GROUPS, 1, IFACE), 0, GRID_BLOCKS * CYCLE - 1)
    first = first.at[0, 0, 0, 0].set(GRID_BLOCKS * CYCLE - 2)
    return jnp.concatenate([first, first + 1], axis=2)


def shard_levels(own_key, extent, cuts, low, top_value):
    def one(position, blocks):
        draws = jax.random.uniform(jax.random.fold_in(jax.random.fold_in(own_key, 6), position), (blocks,), jnp.float32, low / len(cuts), top_value / len(cuts))
        return jnp.repeat(jnp.exp(draws), extent[position] // blocks).reshape((-1,) + (1,) * (len(extent) - position - 1))

    factor_of = one(*cuts[0])
    for cut in cuts[1:]:
        factor_of = factor_of * one(*cut)
    return factor_of


def gaussian(stream_key, extent, scale, bound, cuts=(), held_as=jnp.bfloat16):
    entries = scale * jax.random.normal(stream_key, extent, jnp.float32)
    if cuts:
        entries = entries * shard_levels(stream_key, extent, cuts, -0.22, 0.18)
    return jnp.clip(entries, -bound, bound).astype(held_as)


def setup_inputs(seed: int = 0) -> dict:
    keys = jax.random.split(jax.random.key(seed), 14)
    adjoint_start = gaussian(keys[0], (NVAR, GRID_BLOCKS, NORMAL_CELLS, WALL_LINES), 1.0, 6.0, ((1, 16), (2, 8)), jnp.float32)
    source = gaussian(keys[1], (NVAR, GRID_BLOCKS, NORMAL_CELLS, WALL_LINES), 1.0, 6.0, ((1, 16), (2, 8)), jnp.float32)
    jacobian = draw_jacobian(jax.random.fold_in(keys[13], 71), 0)
    inv_diag = draw_inv_diag(jax.random.fold_in(keys[13], 71), 0)
    lower_prop = draw_lower_prop(jax.random.fold_in(keys[13], 71), 0)
    upper_prop = draw_upper_prop(jax.random.fold_in(keys[13], 71), 0)
    send_cells = draw_send_cells(jax.random.fold_in(keys[13], 71), 0)
    recv_cells = draw_recv_cells(jax.random.fold_in(keys[13], 71), 0)
    face_weight = jnp.clip(0.2 + 0.400000021 * jax.random.uniform(keys[8], (GRID_BLOCKS, GROUPS, GRID_BLOCKS, SLOTS), jnp.float32) ** shard_levels(keys[8], (GRID_BLOCKS, GROUPS, GRID_BLOCKS, SLOTS), ((0, 16), (1, 8)), -0.2, 0.2), 0.2, 0.6)
    cycle_cells = draw_cycle_cells(jax.random.fold_in(keys[13], 71), 0)
    iface_cells = draw_iface_cells(jax.random.fold_in(keys[13], 71), 0)
    iface_donor = draw_iface_donor(jax.random.fold_in(keys[13], 71), 0)
    iface_weight = jnp.clip(0.1 + 0.4 * jax.random.uniform(keys[12], (GRID_BLOCKS, GROUPS, 2, IFACE), jnp.float32) ** shard_levels(keys[12], (GRID_BLOCKS, GROUPS, 2, IFACE), ((0, 16), (1, 8)), -0.2, 0.2), 0.1, 0.5)
    return {"adjoint_start": adjoint_start, "source": source, "jacobian": jacobian, "inv_diag": inv_diag, "lower_prop": lower_prop, "upper_prop": upper_prop, "send_cells": send_cells, "recv_cells": recv_cells, "face_weight": face_weight, "cycle_cells": cycle_cells, "iface_cells": iface_cells, "iface_donor": iface_donor, "iface_weight": iface_weight}


def apply_block(matrix, vector):
    return jnp.einsum("ij...,j...->i...", matrix, vector, precision=lax.Precision.HIGHEST)


def local_coupling(incoming, face_coef, recv_pos, cycle_all, donors, iface_coef, target_pos, cell_count):
    variables = incoming.shape[0]
    summed = jnp.zeros((variables, cell_count), jnp.float32)
    summed = summed.at[:, recv_pos.reshape(-1)].add((incoming * face_coef[None]).reshape(variables, -1))
    picked = jnp.take(cycle_all, donors.reshape(-1), axis=1).reshape(variables, 2, -1)
    summed = summed.at[:, target_pos].add(jnp.sum(picked * iface_coef[None], axis=1))
    return summed


def line_solve(inv_diag, lower_prop, upper_prop, residual):
    inverse_seq = jnp.moveaxis(inv_diag, 3, 0)
    lower_seq = jnp.moveaxis(lower_prop, 3, 0)
    upper_seq = jnp.moveaxis(upper_prop, 3, 0)
    residual_seq = jnp.moveaxis(residual, 2, 0)

    def forward(running, inputs):
        inverse_block, lower_block, residual_here = inputs
        result = apply_block(inverse_block, residual_here) + apply_block(lower_block, running)
        return result, result

    def backward(running, inputs):
        upper_block, sweep_here = inputs
        result = sweep_here + apply_block(upper_block, running)
        return result, result

    start = jnp.zeros(residual_seq.shape[1:], jnp.float32)
    _, sweep_y = lax.scan(forward, start, (inverse_seq, lower_seq, residual_seq))
    _, update = lax.scan(backward, start, (upper_seq, sweep_y), reverse=True)
    return jnp.moveaxis(update, 0, 2)


def reference(adjoint_start, source, jacobian, inv_diag, lower_prop, upper_prop, send_cells, recv_cells, face_weight, cycle_cells, iface_cells, iface_donor, iface_weight):
    variables = adjoint_start.shape[0]
    send_idx = jnp.maximum(send_cells, 0)
    recv_pos = jnp.maximum(recv_cells, 0)
    face_coef = jnp.where(recv_cells >= 0, face_weight, 0.0)
    iface_coef = jnp.where(iface_cells[:, :, None, :] >= 0, iface_weight, 0.0)
    target_pos = jnp.maximum(iface_cells, 0)
    coupling = partial(local_coupling, cell_count=CELLS)
    inner = jax.vmap(coupling, in_axes=(1, 0, 0, 1, 0, 0, 0), out_axes=1)
    outer = jax.vmap(inner, in_axes=(1, 0, 0, None, 0, 0, 0), out_axes=1)
    adjoint = adjoint_start
    for iteration in range(ITERS):
        flat_view = adjoint.reshape(variables, GRID_BLOCKS, GROUPS, CELLS)
        sent = jnp.take_along_axis(flat_view, send_idx.reshape(1, GRID_BLOCKS, GROUPS, GRID_BLOCKS * SLOTS), axis=3)
        sent = sent.reshape(variables, GRID_BLOCKS, GROUPS, GRID_BLOCKS, SLOTS)
        incoming = jnp.transpose(sent, (0, 3, 2, 1, 4))
        cycle_vals = jnp.take_along_axis(flat_view, cycle_cells.reshape(1, GRID_BLOCKS, GROUPS, CYCLE), axis=3)
        cycle_all = jnp.transpose(cycle_vals, (0, 2, 1, 3)).reshape(variables, GROUPS, GRID_BLOCKS * CYCLE)
        coupled = outer(incoming, face_coef, recv_pos, cycle_all, iface_donor, iface_coef, target_pos)
        coupled = coupled.reshape(adjoint.shape)
        residual = source - (apply_block(jacobian, adjoint) - coupled)
        adjoint = adjoint + line_solve(inv_diag, lower_prop, upper_prop, residual)
    return adjoint
```

```python
import jax
import jax.numpy as jnp
from jax import lax
from jax.experimental import pallas as pl
from jax.experimental.pallas import tpu as pltpu
from jax.sharding import PartitionSpec as P

NV = 6
KN = 16
NB = 16
NQ = 8
ITERS = 2
F32 = jnp.float32
BF16 = jnp.bfloat16
LOW = [(i, j) for i in range(NV) for j in range(i + 1)]
UPP = [(i, j) for i in range(NV) for j in range(i, NV)]
LOW_AT = {ij: n for n, ij in enumerate(LOW)}
UPP_AT = {ij: n for n, ij in enumerate(UPP)}
NP = len(LOW)
NH = NV * NV
NPHW = 2 * NP + NH

VMEM = pl.BlockSpec(memory_space=pltpu.VMEM)
ANY = pl.BlockSpec(memory_space=pl.ANY)
SMEM = pl.BlockSpec(memory_space=pltpu.SMEM)


def rows_of(x):
    n = x.size // (16 * 1024)
    x = x.reshape(n, 2, 8, 8, 128)
    return jnp.transpose(x, (0, 1, 3, 2, 4)).reshape(n * 128, 128)


def from_rows(x, n):
    x = x.reshape(n, 2, 8, 8, 128)
    return jnp.transpose(x, (0, 1, 3, 2, 4)).reshape(n, 16, 1024)


def at_k(ref, n, k):
    return ref[pl.ds(n * 128 + (k // 8) * 64 + k % 8, 8, stride=8), :]


def put_k(ref, n, k, value):
    ref[pl.ds(n * 128 + (k // 8) * 64 + k % 8, 8, stride=8), :] = value


def total(terms):
    terms = list(terms)
    while len(terms) > 1:
        nxt = [terms[i] + terms[i + 1] for i in range(0, len(terms) - 1, 2)]
        if len(terms) % 2:
            nxt.append(terms[-1])
        terms = nxt
    return terms[0]


def split_two(x):
    high = x.astype(BF16)
    low = (x - high.astype(F32)).astype(BF16)
    return high, low


def one_hot(index, count):
    rows = lax.broadcasted_iota(jnp.int32, (count, index.shape[1]), 0)
    return jnp.where(rows == index, 1.0, 0.0).astype(BF16)


def stage_table(table, x_ref, v, rows):
    t = table.T
    t = jnp.concatenate([t[:64], t[64:]], axis=1)
    high, low = split_two(t)
    x_ref[pl.ds(v * 64, 64), 0 : 2 * rows] = high
    x_ref[pl.ds(v * 64, 64), 2 * rows : 4 * rows] = low


def pick(x_ref, cell, rows):
    lane = jnp.bitwise_and(cell, 127)
    row = jnp.right_shift(cell, 7)
    key = jnp.right_shift(lane, 6) * rows + row
    low = jnp.bitwise_and(lane, 63)
    hot = one_hot(key, 2 * rows)
    hot = jnp.concatenate([hot, hot], axis=0)
    t = jnp.dot(x_ref[:, : 4 * rows], hot, preferred_element_type=F32)
    mask = lax.broadcasted_iota(jnp.int32, (64, cell.shape[1]), 0) == low
    return [
        jnp.sum(jnp.where(mask, t[v * 64 : (v + 1) * 64], 0.0), axis=0, keepdims=True) for v in range(NV)
    ]


def gather_all(cells_ref, send_ref, cycle_ref, out_ref, x_ref):
    for v in range(NV):
        stage_table(cells_ref[pl.ds(v * 128, 128), :], x_ref, v, 128)

    def face(p, carry):
        cell = jnp.maximum(send_ref[pl.ds(p, 1), :], 0)
        got = pick(x_ref, cell, 128)
        for v in range(NV):
            for c in range(4):
                out_ref[p, c * 12 + v : c * 12 + v + 1, :] = got[v][:, c * 128 : (c + 1) * 128]
        return carry

    lax.fori_loop(0, NB, face, 0)
    got = pick(x_ref, cycle_ref[...], 128)
    for v in range(NV):
        for c in range(4):
            r = c * 12 + 6 + v
            piece = jnp.broadcast_to(got[v][:, c * 128 : (c + 1) * 128][None], (NB, 1, 128))
            out_ref[:, r : r + 1, :] = piece


def first_gather_kernel(start_ref, send_ref, cycle_ref, out_ref, cells_ref, x_ref):
    for v in range(NV):
        for k in range(KN):
            cells_ref[pl.ds(v * 128 + k * 8, 8), :] = at_k(start_ref, v, k)
    gather_all(cells_ref, send_ref, cycle_ref, out_ref, x_ref)


def propagator_kernel(low_ref, upp_ref, out_ref, g_ref):
    def lower(k):
        return {ij: at_k(low_ref, ij[0] * NV + ij[1], k) for ij in LOW}

    def upper(k):
        return {ij: at_k(upp_ref, ij[0] * NV + ij[1], k) for ij in UPP}

    def g_at(k, ij):
        return pl.ds((k * NP + LOW_AT[ij]) * 8, 8)

    for j in range(NV):
        col = None
        for k in range(KN):
            if k == 0:
                col = {i: at_k(low_ref, i * NV + j, 0) for i in range(j, NV)}
            else:
                col = {
                    i: total(at_k(low_ref, i * NV + m, k) * col[m] for m in range(j, i + 1)) for i in range(j, NV)
                }
            for i in range(j, NV):
                g_ref[g_at(k, (i, j)), :] = col[i]
        for i in range(j, NV):
            out_ref[pl.ds(LOW_AT[(i, j)] * 8, 8), :] = col[i]

    for j in range(NV):
        hcol = {i: g_ref[g_at(KN - 1, (i, j)), :] for i in range(j, NV)}
        hcol.update({i: jnp.zeros((8, 128), F32) for i in range(j)})
        wcol = {i: at_k(upp_ref, i * NV + j, KN - 1) for i in range(j + 1)}
        for k in range(KN - 2, -1, -1):
            u = {(i, m): at_k(upp_ref, i * NV + m, k) for (i, m) in UPP}
            new_h = {}
            for i in range(NV):
                terms = [u[(i, m)] * hcol[m] for m in range(i, NV)]
                if i >= j:
                    terms.append(g_ref[g_at(k, (i, j)), :])
                new_h[i] = total(terms)
            wcol = {i: total(u[(i, m)] * wcol[m] for m in range(i, j + 1)) for i in range(j + 1)}
            hcol = new_h
        for i in range(NV):
            out_ref[pl.ds((NP + i * NV + j) * 8, 8), :] = hcol[i]
        for i in range(j + 1):
            out_ref[pl.ds((NP + NH + UPP_AT[(i, j)]) * 8, 8), :] = wcol[i]


def residual_kernel(
    recv_ref,
    recv_cells_ref,
    face_weight_ref,
    iface_cells_ref,
    donor_ref,
    iface_weight_ref,
    cells_ref,
    source_ref,
    jac_any,
    inv_any,
    low_any,
    upp_any,
    bound_ref,
    drive_ref,
    jac_ref,
    inv_ref,
    low_ref,
    upp_ref,
    acc_ref,
    x_ref,
    y_ref,
    sem,
):
    copies = [
        pltpu.make_async_copy(src, dst, sem.at[n])
        for n, (src, dst) in enumerate(
            [(jac_any, jac_ref), (inv_any, inv_ref), (low_any, low_ref), (upp_any, upp_ref)]
        )
    ]
    for copy in copies:
        copy.start()

    def add_slots(values, target):
        row = jnp.right_shift(target, 7)
        lane = jnp.bitwise_and(target, 127)
        hot_row = one_hot(jnp.bitwise_and(row, 63), 64)
        hot_lane = one_hot(jnp.right_shift(row, 6) * 128 + lane, 256)
        parts = []
        for v in range(NV):
            wide = jnp.broadcast_to(values[v], (16, values[v].shape[1]))
            parts.append(split_two(wide))
        left = jnp.concatenate(
            [hot_row * jnp.concatenate([parts[v][h]] * 4, axis=0) for h in range(2) for v in range(NV)], axis=0
        )
        acc_ref[...] += lax.dot_general(
            left, hot_lane, (((1,), (1,)), ((), ())), preferred_element_type=F32
        )

    acc_ref[...] = jnp.zeros_like(acc_ref)

    def face(p, carry):
        weight = face_weight_ref[pl.ds(p, 1), :]
        values = []
        for v in range(NV):
            got = jnp.concatenate(
                [recv_ref[pl.ds(p * 48 + c * 12 + v, 1), :] for c in range(4)], axis=1
            )
            values.append(got * weight)
        add_slots(values, recv_cells_ref[pl.ds(p, 1), :])
        return carry

    lax.fori_loop(0, NB, face, 0)

    for v in range(NV):
        stage_table(recv_ref[pl.ds(6 + v, 64, stride=12), :], x_ref, v, 64)
    first = pick(x_ref, donor_ref[0:1, :], 64)
    second = pick(x_ref, donor_ref[1:2, :], 64)
    w0 = iface_weight_ref[0:1, :]
    w1 = iface_weight_ref[1:2, :]
    add_slots([first[v] * w0 + second[v] * w1 for v in range(NV)], iface_cells_ref[...])

    for copy in copies:
        copy.wait()

    y = None
    for k in range(KN):
        a = [cells_ref[pl.ds(v * 128 + k * 8, 8), :] for v in range(NV)]
        r = []
        half, row = k // 8, (k % 8) * 8
        lanes = slice(half * 128, half * 128 + 128)
        for i in range(NV):
            coupled = acc_ref[i * 64 + row : i * 64 + row + 8, lanes]
            coupled = coupled + acc_ref[384 + i * 64 + row : 384 + i * 64 + row + 8, lanes]
            product = total(at_k(jac_ref, i * NV + j, k) * a[j] for j in range(NV))
            r.append(at_k(source_ref, i, k) - (product - coupled))
        d = [total(at_k(inv_ref, i * NV + j, k) * r[j] for j in range(NV)) for i in range(NV)]
        if k == 0:
            y = d
        else:
            y = [d[i] + total(at_k(low_ref, i * NV + j, k) * y[j] for j in range(i + 1)) for i in range(NV)]
        for i in range(NV):
            drive_ref[pl.ds(i * 128 + k * 8, 8), :] = d[i]
            y_ref[pl.ds(i * 128 + k * 8, 8), :] = y[i]
    u = y
    for k in range(KN - 2, -1, -1):
        u = [
            y_ref[pl.ds(i * 128 + k * 8, 8), :]
            + total(at_k(upp_ref, i * NV + j, k) * u[j] for j in range(i, NV))
            for i in range(NV)
        ]
    for i in range(NV):
        for q in range(NQ):
            bound_ref[q, pl.ds(i * 8, 8), :] = y[i]
            bound_ref[q, pl.ds(48 + i * 8, 8), :] = u[i]


def solve_lines(q_ref, bound_ref, phw_ref, drive_ref, low_ref, upp_ref, cells_ref, yin_ref, uin_ref, y_ref, put):
    zero = jnp.zeros((8, 128), F32)

    def p_at(p, i, j):
        return phw_ref[p, pl.ds(LOW_AT[(i, j)] * 8, 8), :]

    def h_at(p, i, j):
        return phw_ref[p, pl.ds((NP + i * NV + j) * 8, 8), :]

    def w_at(p, i, j):
        return phw_ref[p, pl.ds((NP + NH + UPP_AT[(i, j)]) * 8, 8), :]

    y = [zero] * NV
    for p in range(NQ):
        for i in range(NV):
            yin_ref[p, pl.ds(i * 8, 8), :] = y[i]
        if p + 1 < NQ:
            y = [
                bound_ref[p, pl.ds(i * 8, 8), :] + total(p_at(p, i, j) * y[j] for j in range(i + 1))
                for i in range(NV)
            ]
    u = [zero] * NV
    for p in range(NQ - 1, -1, -1):
        for i in range(NV):
            uin_ref[p, pl.ds(i * 8, 8), :] = u[i]
        if p > 0:
            yp = [yin_ref[p, pl.ds(i * 8, 8), :] for i in range(NV)]
            u = [
                bound_ref[p, pl.ds(48 + i * 8, 8), :]
                + total(h_at(p, i, j) * yp[j] for j in range(NV))
                + total(w_at(p, i, j) * u[j] for j in range(i, NV))
                for i in range(NV)
            ]
    q = q_ref[0]
    y = [yin_ref[q, pl.ds(i * 8, 8), :] for i in range(NV)]
    u = [uin_ref[q, pl.ds(i * 8, 8), :] for i in range(NV)]
    for k in range(KN):
        y = [
            drive_ref[pl.ds(i * 128 + k * 8, 8), :]
            + total(at_k(low_ref, i * NV + j, k) * y[j] for j in range(i + 1))
            for i in range(NV)
        ]
        for i in range(NV):
            y_ref[pl.ds(i * 128 + k * 8, 8), :] = y[i]
    for k in range(KN - 1, -1, -1):
        u = [
            y_ref[pl.ds(i * 128 + k * 8, 8), :]
            + total(at_k(upp_ref, i * NV + j, k) * u[j] for j in range(i, NV))
            for i in range(NV)
        ]
        for i in range(NV):
            put(i, k, cells_ref[pl.ds(i * 128 + k * 8, 8), :] + u[i])


def update_kernel(
    q_ref, bound_ref, phw_ref, drive_ref, low_ref, upp_ref, cells_ref, send_ref, cycle_ref,
    out_ref, new_ref, yin_ref, uin_ref, y_ref, x_ref,
):
    def put(i, k, value):
        new_ref[pl.ds(i * 128 + k * 8, 8), :] = value

    solve_lines(q_ref, bound_ref, phw_ref, drive_ref, low_ref, upp_ref, cells_ref, yin_ref, uin_ref, y_ref, put)
    gather_all(new_ref, send_ref, cycle_ref, out_ref, x_ref)


def final_kernel(
    q_ref, bound_ref, phw_ref, drive_ref, low_ref, upp_ref, cells_ref, new_ref, yin_ref, uin_ref, y_ref
):
    def put(i, k, value):
        put_k(new_ref, i, k, value)

    solve_lines(q_ref, bound_ref, phw_ref, drive_ref, low_ref, upp_ref, cells_ref, yin_ref, uin_ref, y_ref, put)


def f32(*shape):
    return jax.ShapeDtypeStruct(shape, F32)


PARAMS = pltpu.CompilerParams(vmem_limit_bytes=40 * 1024 * 1024)


def body(
    adjoint_start, source, jacobian, inv_diag, lower_prop, upper_prop, send_cells, recv_cells,
    face_weight, cycle_cells, iface_cells, iface_donor, iface_weight,
):
    start = rows_of(adjoint_start)
    src = rows_of(source)
    jac = rows_of(jacobian)
    inv = rows_of(inv_diag)
    low = rows_of(lower_prop)
    upp = rows_of(upper_prop)
    send = send_cells.reshape(NB, 512)
    recv_at = recv_cells.reshape(NB, 512)
    weight = face_weight.reshape(NB, 512)
    cycle = cycle_cells.reshape(1, 512)
    iface_at = iface_cells.reshape(1, 512)
    donor = iface_donor.reshape(2, 512)
    iface_w = iface_weight.reshape(2, 512)
    q = lax.axis_index("line").reshape(1).astype(jnp.int32)

    phw = pl.pallas_call(
        propagator_kernel,
        out_shape=f32(NPHW * 8, 128),
        in_specs=[VMEM] * 2,
        out_specs=VMEM,
        scratch_shapes=[pltpu.VMEM((KN * NP * 8, 128), F32)],
        compiler_params=PARAMS,
        name="propagators",
    )(low, upp)
    phw_all = lax.all_gather(phw, "line", axis=0)

    outgoing, cells = pl.pallas_call(
        first_gather_kernel,
        out_shape=(f32(NB, 48, 128), f32(NV * 128, 128)),
        in_specs=[VMEM] * 3,
        out_specs=(VMEM, VMEM),
        scratch_shapes=[pltpu.VMEM((384, 512), BF16)],
        compiler_params=PARAMS,
        name="first_gather",
    )(start, send, cycle)

    mats = [pltpu.VMEM((NV * NV * 128, 128), F32)] * 4
    line_scratch = [
        pltpu.VMEM((NQ, 48, 128), F32),
        pltpu.VMEM((NQ, 48, 128), F32),
        pltpu.VMEM((NV * 128, 128), F32),
    ]
    for iteration in range(ITERS):
        incoming = lax.all_to_all(outgoing, "block", split_axis=0, concat_axis=0, tiled=True)
        bound, drive = pl.pallas_call(
            residual_kernel,
            out_shape=(f32(NQ, 96, 128), f32(NV * 128, 128)),
            in_specs=[VMEM] * 8 + [ANY] * 4,
            out_specs=(VMEM, VMEM),
            scratch_shapes=mats
            + [
                pltpu.VMEM((768, 256), F32),
                pltpu.VMEM((384, 256), BF16),
                pltpu.VMEM((NV * 128, 128), F32),
                pltpu.SemaphoreType.DMA((4,)),
            ],
            compiler_params=PARAMS,
            name="residual",
        )(incoming.reshape(NB * 48, 128), recv_at, weight, iface_at, donor, iface_w, cells, src, jac, inv, low, upp)
        bound_all = lax.all_to_all(bound, "line", split_axis=0, concat_axis=0, tiled=True)
        if iteration + 1 < ITERS:
            outgoing, cells = pl.pallas_call(
                update_kernel,
                out_shape=(f32(NB, 48, 128), f32(NV * 128, 128)),
                in_specs=[SMEM] + [VMEM] * 8,
                out_specs=(VMEM, VMEM),
                scratch_shapes=line_scratch + [pltpu.VMEM((384, 512), BF16)],
                compiler_params=PARAMS,
                name="update",
            )(q, bound_all, phw_all, drive, low, upp, cells, send, cycle)
        else:
            result = pl.pallas_call(
                final_kernel,
                out_shape=f32(NV * 128, 128),
                in_specs=[SMEM] + [VMEM] * 6,
                out_specs=VMEM,
                scratch_shapes=line_scratch,
                compiler_params=PARAMS,
                name="final_update",
            )(q, bound_all, phw_all, drive, low, upp, cells)
    return from_rows(result, NV)[:, None]


def solution(mesh):
    cell = P(None, "block", "line", None)
    matrix = P(None, None, "block", "line", None)
    slots = P("block", "line", None, None)
    flat = P("block", "line", None)
    placed = (cell, cell, matrix, matrix, matrix, matrix, slots, slots, slots, flat, flat, slots, slots)
    return jax.shard_map(body, mesh=mesh, in_specs=placed, out_specs=cell, check_vma=False)
```

```python
from functools import partial

import jax
import jax.numpy as jnp
from jax import lax
from jax.experimental import pallas as pl
from jax.experimental.pallas import tpu as pltpu
from jax.sharding import PartitionSpec as P

NV = 6
KN = 16
NB = 16
NQ = 8
ITERS = 2
ORDER = True
PICK = 2 * 768 * 256 * 17 * 512
F32 = jnp.float32
BF16 = jnp.bfloat16
LOW = [(i, j) for i in range(NV) for j in range(i + 1)]
UPP = [(i, j) for i in range(NV) for j in range(i, NV)]
LOW_AT = {ij: n for n, ij in enumerate(LOW)}
UPP_AT = {ij: n for n, ij in enumerate(UPP)}
NP = len(LOW)
NH = NV * NV
NPHW = 2 * NP + NH
ROWS = 80
ENDS = 16
BOTH = ROWS + ENDS

VMEM = pl.BlockSpec(memory_space=pltpu.VMEM)
HBM = pl.BlockSpec(memory_space=pltpu.HBM)
SMEM = pl.BlockSpec(memory_space=pltpu.SMEM)


def rows_of(x):
    n = x.size // (16 * 1024)
    x = x.reshape(n, 2, 8, 8, 128)
    return jnp.transpose(x, (0, 1, 3, 2, 4)).reshape(n * 128, 128)


def from_rows(x, n):
    x = x.reshape(n, 2, 8, 8, 128)
    return jnp.transpose(x, (0, 1, 3, 2, 4)).reshape(n, 16, 1024)


def at_k(ref, n, k):
    return ref[pl.ds(n * 128 + (k // 8) * 64 + k % 8, 8, stride=8), :]


def put_k(ref, n, k, value):
    ref[pl.ds(n * 128 + (k // 8) * 64 + k % 8, 8, stride=8), :] = value


def total(terms):
    terms = list(terms)
    while len(terms) > 1:
        nxt = [terms[i] + terms[i + 1] for i in range(0, len(terms) - 1, 2)]
        if len(terms) % 2:
            nxt.append(terms[-1])
        terms = nxt
    return terms[0]


def split_two(x):
    high = x.astype(BF16)
    low = (x - high.astype(F32)).astype(BF16)
    return high, low


def one_hot(index, count):
    rows = lax.broadcasted_iota(jnp.int32, (count, index.shape[1]), 0)
    return jnp.where(rows == index, 1.0, 0.0).astype(BF16)


def stage_table(table, x_ref, v, rows):
    t = table.T
    t = jnp.concatenate([t[:64], t[64:]], axis=1)
    high, low = split_two(t)
    x_ref[v * 64 : v * 64 + 64, 0 : 2 * rows] = high
    x_ref[384 + v * 64 : 384 + v * 64 + 64, 0 : 2 * rows] = low


def pick(x_ref, cell, rows):
    lane = jnp.bitwise_and(cell, 127)
    row = jnp.right_shift(cell, 7)
    key = jnp.right_shift(lane, 6) * rows + row
    low = jnp.bitwise_and(lane, 63)
    t = jnp.dot(x_ref[:, : 2 * rows], one_hot(key, 2 * rows), preferred_element_type=F32)
    t = t[:384] + t[384:]
    mask = lax.broadcasted_iota(jnp.int32, (64, cell.shape[1]), 0) == low
    return [
        jnp.sum(jnp.where(mask, t[v * 64 : (v + 1) * 64], 0.0), axis=0, keepdims=True) for v in range(NV)
    ]


def gather_all(cells_ref, send_ref, cycle_ref, out_ref, x_ref):
    for v in range(NV):
        stage_table(cells_ref[pl.ds(v * 128, 128), :], x_ref, v, 128)
    for p in range(NB):
        got = pick(x_ref, jnp.maximum(send_ref[p : p + 1, :], 0), 128)
        for v in range(NV):
            for c in range(4):
                out_ref[p, c * 12 + v : c * 12 + v + 1, :] = got[v][:, c * 128 : (c + 1) * 128]
    got = pick(x_ref, cycle_ref[...], 128)
    for v in range(NV):
        for c in range(4):
            r = c * 12 + 6 + v
            piece = jnp.broadcast_to(got[v][:, c * 128 : (c + 1) * 128][None], (NB, 1, 128))
            out_ref[:, r : r + 1, :] = piece


def first_gather_kernel(start_ref, send_ref, cycle_ref, out_ref, cells_ref, x_ref):
    for v in range(NV):
        for k in range(KN):
            cells_ref[pl.ds((v * KN + k) * 8, 8), :] = at_k(start_ref, v, k)
    gather_all(cells_ref, send_ref, cycle_ref, out_ref, x_ref)


def prepare_kernel(low_ref, upp_ref, out_ref, lowc_ref, uppc_ref, g_ref):
    for i, j in LOW:
        for k in range(KN):
            lowc_ref[pl.ds((LOW_AT[(i, j)] * KN + k) * 8, 8), :] = at_k(low_ref, i * NV + j, k)
    for i, j in UPP:
        for k in range(KN):
            uppc_ref[pl.ds((UPP_AT[(i, j)] * KN + k) * 8, 8), :] = at_k(upp_ref, i * NV + j, k)

    def low(k, i, j):
        return lowc_ref[pl.ds((LOW_AT[(i, j)] * KN + k) * 8, 8), :]

    def upp(k, i, j):
        return uppc_ref[pl.ds((UPP_AT[(i, j)] * KN + k) * 8, 8), :]

    def g_at(k, i, j):
        return pl.ds((k * NP + LOW_AT[(i, j)]) * 8, 8)

    def send(n, value):
        out_ref[pl.ds(n, NQ, stride=ROWS), :] = value

    for j in range(NV):
        col = {i: low(0, i, j) for i in range(j, NV)}
        for i in range(j, NV):
            g_ref[g_at(0, i, j), :] = col[i]
        for k in range(1, KN):
            col = {i: total(low(k, i, m) * col[m] for m in range(j, i + 1)) for i in range(j, NV)}
            for i in range(j, NV):
                g_ref[g_at(k, i, j), :] = col[i]
        for i in range(j, NV):
            send(LOW_AT[(i, j)], col[i])

    for j in range(NV):
        hcol = {i: g_ref[g_at(KN - 1, i, j), :] if i >= j else jnp.zeros((8, 128), F32) for i in range(NV)}
        wcol = {i: upp(KN - 1, i, j) for i in range(j + 1)}
        for k in range(KN - 2, -1, -1):
            u = {(i, m): upp(k, i, m) for (i, m) in UPP}
            wcol = {i: total(u[(i, m)] * wcol[m] for m in range(i, j + 1)) for i in range(j + 1)}
            new_h = {}
            for i in range(NV):
                terms = [u[(i, m)] * hcol[m] for m in range(i, NV)]
                if i >= j:
                    terms.append(g_ref[g_at(k, i, j), :])
                new_h[i] = total(terms)
            hcol = new_h
        for i in range(NV):
            send(NP + i * NV + j, hcol[i])
        for i in range(j + 1):
            send(NP + NH + UPP_AT[(i, j)], wcol[i])


def residual_kernel(
    with_products,
    recv_ref,
    recv_cells_ref,
    face_weight_ref,
    iface_cells_ref,
    donor_ref,
    iface_weight_ref,
    cells_ref,
    source_ref,
    low_ref,
    upp_ref,
    jac_ref,
    inv_ref,
    *refs,
):
    if with_products:
        products_ref, *refs = refs
    bound_ref, drive_ref, acc_ref, x_ref, y_ref = refs
    stride = BOTH if with_products else ENDS
    if with_products:
        for q in range(NQ):
            bound_ref[q * BOTH : q * BOTH + ROWS, :] = products_ref[q * ROWS : (q + 1) * ROWS, :]
    def add_slots(values, target):
        row = jnp.right_shift(target, 7)
        lane = jnp.bitwise_and(target, 127)
        hot_row = one_hot(jnp.bitwise_and(row, 63), 64)
        hot_lane = one_hot(jnp.right_shift(row, 6) * 128 + lane, 256)
        parts = []
        for v in range(NV):
            wide = jnp.broadcast_to(values[v], (16, values[v].shape[1]))
            parts.append(split_two(wide))
        left = jnp.concatenate(
            [hot_row * jnp.concatenate([parts[v][h]] * 4, axis=0) for h in range(2) for v in range(NV)], axis=0
        )
        acc_ref[...] += lax.dot_general(
            left, hot_lane, (((1,), (1,)), ((), ())), preferred_element_type=F32
        )

    acc_ref[...] = jnp.zeros_like(acc_ref)
    for p in range(NB):
        weight = face_weight_ref[p : p + 1, :]
        values = []
        for v in range(NV):
            rows = [p * 48 + c * 12 + v for c in range(4)]
            values.append(jnp.concatenate([recv_ref[r : r + 1, :] for r in rows], axis=1) * weight)
        add_slots(values, recv_cells_ref[p : p + 1, :])

    for v in range(NV):
        stage_table(recv_ref[pl.ds(6 + v, 64, stride=12), :], x_ref, v, 64)
    first = pick(x_ref, donor_ref[0:1, :], 64)
    second = pick(x_ref, donor_ref[1:2, :], 64)
    w0 = iface_weight_ref[0:1, :]
    w1 = iface_weight_ref[1:2, :]
    add_slots([first[v] * w0 + second[v] * w1 for v in range(NV)], iface_cells_ref[...])

    y = None
    for k in range(KN):
        a = [cells_ref[pl.ds(v * 128 + k * 8, 8), :] for v in range(NV)]
        r = []
        half, row = k // 8, (k % 8) * 8
        lanes = slice(half * 128, half * 128 + 128)
        for i in range(NV):
            coupled = acc_ref[i * 64 + row : i * 64 + row + 8, lanes]
            coupled = coupled + acc_ref[384 + i * 64 + row : 384 + i * 64 + row + 8, lanes]
            product = total(at_k(jac_ref, i * NV + j, k) * a[j] for j in range(NV))
            r.append(at_k(source_ref, i, k) - (product - coupled))
        d = [total(at_k(inv_ref, i * NV + j, k) * r[j] for j in range(NV)) for i in range(NV)]
        if k == 0:
            y = d
        else:
            y = [d[i] + total(low_ref[pl.ds((LOW_AT[(i, j)] * KN + k) * 8, 8), :] * y[j] for j in range(i + 1)) for i in range(NV)]
        for i in range(NV):
            drive_ref[pl.ds(i * 128 + k * 8, 8), :] = d[i]
            y_ref[pl.ds(i * 128 + k * 8, 8), :] = y[i]
    u = y
    for k in range(KN - 2, -1, -1):
        u = [
            y_ref[pl.ds(i * 128 + k * 8, 8), :]
            + total(upp_ref[pl.ds((UPP_AT[(i, j)] * KN + k) * 8, 8), :] * u[j] for j in range(i, NV))
            for i in range(NV)
        ]
    for i in range(NV):
        bound_ref[pl.ds(stride - ENDS + i, NQ, stride=stride), :] = y[i]
        bound_ref[pl.ds(stride - ENDS + NV + i, NQ, stride=stride), :] = u[i]


def boundary_kernel(stride, phw_ref, *refs):
    *bounds, out_ref = refs
    bound_ref = bounds[0] if bounds else phw_ref

    def end_at(p, n):
        at = (p + 1) * stride - ENDS + n
        return bound_ref[at : at + 1, :]

    def factor(p, n):
        return phw_ref[p * BOTH + n : p * BOTH + n + 1, :]

    zero = jnp.zeros((1, 128), F32)
    y = [zero] * NV
    entering = []
    for p in range(NQ):
        entering.append(y)
        for i in range(NV):
            out_ref[p * ENDS + i : p * ENDS + i + 1, :] = y[i]
        if p + 1 < NQ:
            y = [
                end_at(p, i)
                + total(factor(p, LOW_AT[(i, j)]) * y[j] for j in range(i + 1))
                for i in range(NV)
            ]
    u = [zero] * NV
    for p in range(NQ - 1, -1, -1):
        for i in range(NV):
            out_ref[p * ENDS + NV + i : p * ENDS + NV + i + 1, :] = u[i]
        if p > 0:
            y = entering[p]
            known = [
                end_at(p, NV + i) + total(factor(p, NP + i * NV + j) * y[j] for j in range(NV))
                for i in range(NV)
            ]
            u = [
                known[i] + total(factor(p, NP + NH + UPP_AT[(i, j)]) * u[j] for j in range(i, NV))
                for i in range(NV)
            ]


def solve_lines(enter_ref, drive_ref, low_ref, upp_ref, cells_ref, y_ref, put):
    y = [enter_ref[pl.ds(i, NQ, stride=ENDS), :] for i in range(NV)]
    u = [enter_ref[pl.ds(NV + i, NQ, stride=ENDS), :] for i in range(NV)]
    for k in range(KN):
        y = [
            drive_ref[pl.ds(i * 128 + k * 8, 8), :]
            + total(low_ref[pl.ds((LOW_AT[(i, j)] * KN + k) * 8, 8), :] * y[j] for j in range(i + 1))
            for i in range(NV)
        ]
        for i in range(NV):
            y_ref[pl.ds(i * 128 + k * 8, 8), :] = y[i]
    for k in range(KN - 1, -1, -1):
        u = [
            y_ref[pl.ds(i * 128 + k * 8, 8), :]
            + total(upp_ref[pl.ds((UPP_AT[(i, j)] * KN + k) * 8, 8), :] * u[j] for j in range(i, NV))
            for i in range(NV)
        ]
        for i in range(NV):
            put(i, k, cells_ref[pl.ds(i * 128 + k * 8, 8), :] + u[i])


def update_kernel(enter_ref, drive_ref, low_ref, upp_ref, cells_ref, send_ref, cycle_ref, out_ref, new_ref, y_ref, x_ref):
    def put(i, k, value):
        new_ref[pl.ds(i * 128 + k * 8, 8), :] = value

    solve_lines(enter_ref, drive_ref, low_ref, upp_ref, cells_ref, y_ref, put)
    gather_all(new_ref, send_ref, cycle_ref, out_ref, x_ref)


def final_kernel(enter_ref, drive_ref, low_ref, upp_ref, cells_ref, new_ref, y_ref):
    def put(i, k, value):
        put_k(new_ref, i, k, value)

    solve_lines(enter_ref, drive_ref, low_ref, upp_ref, cells_ref, y_ref, put)


def f32(*shape):
    return jax.ShapeDtypeStruct(shape, F32)


PARAMS = pltpu.CompilerParams(vmem_limit_bytes=20 * 1024 * 1024)


def body(
    adjoint_start, source, jacobian, inv_diag, lower_prop, upper_prop, send_cells, recv_cells,
    face_weight, cycle_cells, iface_cells, iface_donor, iface_weight,
):
    start = rows_of(adjoint_start)
    src = rows_of(source)
    jac = rows_of(jacobian)
    inv = rows_of(inv_diag)
    low = rows_of(lower_prop)
    upp = rows_of(upper_prop)
    send = send_cells.reshape(NB, 512)
    recv_at = recv_cells.reshape(NB, 512)
    weight = face_weight.reshape(NB, 512)
    cycle = cycle_cells.reshape(1, 512)
    iface_at = iface_cells.reshape(1, 512)
    donor = iface_donor.reshape(2, 512)
    iface_w = iface_weight.reshape(2, 512)

    def call(kernel, name, out, operands, scratch=(), flops=0):
        size = sum(4 * x.size for x in operands)
        return pl.pallas_call(
            kernel,
            out_shape=out,
            in_specs=[VMEM] * len(operands),
            out_specs=jax.tree.map(lambda _: VMEM, out),
            scratch_shapes=list(scratch),
            compiler_params=PARAMS,
            cost_estimate=pl.CostEstimate(flops=flops, bytes_accessed=size, transcendentals=0),
            name=name,
        )(*operands)

    def exchange(x, axis, parts):
        x = x.reshape(parts, x.size // (parts * 128), 128)
        return lax.all_to_all(x, axis, split_axis=0, concat_axis=0, tiled=True)

    field = f32(NV * 128, 128)
    faces = f32(NB, 48, 128)
    table = pltpu.VMEM((768, 256), BF16)
    lines = pltpu.VMEM((NV * 128, 128), F32)
    outgoing, cells = call(first_gather_kernel, "first_gather", (faces, field), (start, send, cycle), [table], PICK)
    for iteration in range(ITERS):
        incoming = exchange(outgoing, "block", NB)
        operands = (recv_at, weight, iface_at, donor, iface_w, cells, src)
        stride = ENDS
        if iteration == 0:
            if ORDER:
                incoming, low, upp = lax.optimization_barrier((incoming, low, upp))
            phw, lowc, uppc = call(
                prepare_kernel,
                "prepare",
                (f32(NQ * ROWS, 128), f32(NP * 128, 128), f32(NP * 128, 128)),
                (low, upp),
                [pltpu.VMEM((KN * NP * 8, 128), F32)],
            )
            stride = BOTH
        operands = (incoming.reshape(NB * 48, 128),) + operands + (lowc, uppc, jac, inv)
        if iteration == 0:
            operands += (phw,)
        bound, drive = call(
            partial(residual_kernel, iteration == 0),
            "residual",
            (f32(NQ * stride, 128), field),
            operands,
            [pltpu.VMEM((768, 256), F32), pltpu.VMEM((768, 128), BF16), lines],
            PICK,
        )
        bound = exchange(bound, "line", NQ).reshape(NQ * stride, 128)
        if iteration == 0:
            products = bound
            operands = (bound,)
        else:
            operands = (products, bound)
        enter = call(partial(boundary_kernel, stride), "boundary", f32(NQ * ENDS, 128), operands)
        enter = exchange(enter, "line", NQ).reshape(NQ * ENDS, 128)
        operands = (enter, drive, lowc, uppc, cells)
        if iteration + 1 < ITERS:
            outgoing, cells = call(update_kernel, "update", (faces, field), operands + (send, cycle), [lines, table], PICK)
        else:
            result = call(final_kernel, "final_update", field, operands, [lines])
    return from_rows(result, NV)[:, None]


def solution(mesh):
    cell = P(None, "block", "line", None)
    matrix = P(None, None, "block", "line", None)
    slots = P("block", "line", None, None)
    flat = P("block", "line", None)
    placed = (cell, cell, matrix, matrix, matrix, matrix, slots, slots, slots, flat, flat, slots, slots)
    return jax.shard_map(body, mesh=mesh, in_specs=placed, out_specs=cell, check_vma=False)
```

```python
from functools import partial

import jax
import jax.numpy as jnp
from jax import lax
from jax.experimental import pallas as pl
from jax.experimental.pallas import tpu as pltpu
from jax.sharding import PartitionSpec as P

NV = 6
KN = 16
NB = 16
NQ = 8
ITERS = 2
FIRST_HINT = 6
PICK = 2 * 768 * 256 * 17 * 512
F32 = jnp.float32
BF16 = jnp.bfloat16
LOW = [(i, j) for i in range(NV) for j in range(i + 1)]
UPP = [(i, j) for i in range(NV) for j in range(i, NV)]
LOW_AT = {ij: n for n, ij in enumerate(LOW)}
UPP_AT = {ij: n for n, ij in enumerate(UPP)}
NP = len(LOW)
NH = NV * NV
NPHW = 2 * NP + NH
ROWS = 80
ENDS = 16
BOTH = ROWS + ENDS

VMEM = pl.BlockSpec(memory_space=pltpu.VMEM)
HBM = pl.BlockSpec(memory_space=pltpu.HBM)
SMEM = pl.BlockSpec(memory_space=pltpu.SMEM)


def rows_of(x):
    n = x.size // (16 * 1024)
    x = x.reshape(n, 2, 8, 8, 128)
    return jnp.transpose(x, (0, 1, 3, 2, 4)).reshape(n * 128, 128)


def from_rows(x, n):
    x = x.reshape(n, 2, 8, 8, 128)
    return jnp.transpose(x, (0, 1, 3, 2, 4)).reshape(n, 16, 1024)


def at_k(ref, n, k):
    return ref[pl.ds(n * 128 + (k // 8) * 64 + k % 8, 8, stride=8), :]


def put_k(ref, n, k, value):
    ref[pl.ds(n * 128 + (k // 8) * 64 + k % 8, 8, stride=8), :] = value


def total(terms):
    terms = list(terms)
    while len(terms) > 1:
        nxt = [terms[i] + terms[i + 1] for i in range(0, len(terms) - 1, 2)]
        if len(terms) % 2:
            nxt.append(terms[-1])
        terms = nxt
    return terms[0]


def split_two(x):
    high = x.astype(BF16)
    low = (x - high.astype(F32)).astype(BF16)
    return high, low


def one_hot(index, count):
    rows = lax.broadcasted_iota(jnp.int32, (count, index.shape[1]), 0)
    return jnp.where(rows == index, 1.0, 0.0).astype(BF16)


def stage_table(table, x_ref, v, rows):
    t = table.T
    t = jnp.concatenate([t[:64], t[64:]], axis=1)
    high, low = split_two(t)
    x_ref[v * 64 : v * 64 + 64, 0 : 2 * rows] = high
    x_ref[384 + v * 64 : 384 + v * 64 + 64, 0 : 2 * rows] = low


def pick(x_ref, cell, rows):
    lane = jnp.bitwise_and(cell, 127)
    row = jnp.right_shift(cell, 7)
    key = jnp.right_shift(lane, 6) * rows + row
    low = jnp.bitwise_and(lane, 63)
    t = jnp.dot(x_ref[:, : 2 * rows], one_hot(key, 2 * rows), preferred_element_type=F32)
    t = t[:384] + t[384:]
    mask = lax.broadcasted_iota(jnp.int32, (64, cell.shape[1]), 0) == low
    return [
        jnp.sum(jnp.where(mask, t[v * 64 : (v + 1) * 64], 0.0), axis=0, keepdims=True) for v in range(NV)
    ]


def other_block(me_ref, n):
    return jnp.bitwise_and(me_ref[0] + 1 + n, NB - 1)


def gather_all(me_ref, cells_ref, picks_ref, out_ref, x_ref):
    for v in range(NV):
        stage_table(cells_ref[pl.ds(v * 128, 128), :], x_ref, v, 128)
    for n in range(NB - 1):
        p = other_block(me_ref, n)
        got = pick(x_ref, jnp.maximum(picks_ref[pl.ds(p, 1), :], 0), 128)
        for v in range(NV):
            for c in range(4):
                out_ref[p, c * 12 + v : c * 12 + v + 1, :] = got[v][:, c * 128 : (c + 1) * 128]
    got = pick(x_ref, picks_ref[NB : NB + 1, :], 128)
    for v in range(NV):
        for c in range(4):
            r = c * 12 + 6 + v
            piece = jnp.broadcast_to(got[v][:, c * 128 : (c + 1) * 128][None], (NB, 1, 128))
            out_ref[:, r : r + 1, :] = piece


def first_gather_kernel(me_ref, start_ref, picks_ref, out_ref, cells_ref, x_ref):
    for v in range(NV):
        for k in range(KN):
            cells_ref[pl.ds((v * KN + k) * 8, 8), :] = at_k(start_ref, v, k)
    gather_all(me_ref, cells_ref, picks_ref, out_ref, x_ref)


def product_steps(low_ref, upp_ref, lowc_ref, uppc_ref, bound_ref, g_ref, h_ref, w_ref):
    def g_at(k, i, j):
        return pl.ds((k * NP + LOW_AT[(i, j)]) * 8, 8)

    def forward_step(k):
        low = {(i, j): at_k(low_ref, i * NV + j, k) for (i, j) in LOW}
        for i, j in LOW:
            lowc_ref[pl.ds((LOW_AT[(i, j)] * KN + k) * 8, 8), :] = low[(i, j)]
        for j in range(NV):
            before = {m: g_ref[g_at(k - 1, m, j), :] for m in range(j, NV)} if k else None
            for i in range(j, NV):
                g = total(low[(i, m)] * before[m] for m in range(j, i + 1)) if k else low[(i, j)]
                g_ref[g_at(k, i, j), :] = g
                if k == KN - 1:
                    bound_ref[pl.ds(LOW_AT[(i, j)], NQ, stride=BOTH), :] = g

    def backward_step(k):
        upp = {(i, j): at_k(upp_ref, i * NV + j, k) for (i, j) in UPP}
        for i, j in UPP:
            uppc_ref[pl.ds((UPP_AT[(i, j)] * KN + k) * 8, 8), :] = upp[(i, j)]
        last = k == KN - 1
        for j in range(NV):
            old_w = None if last else {m: w_ref[pl.ds(UPP_AT[(m, j)] * 8, 8), :] for m in range(j + 1)}
            for i in range(j + 1):
                w = upp[(i, j)] if last else total(upp[(i, m)] * old_w[m] for m in range(i, j + 1))
                w_ref[pl.ds(UPP_AT[(i, j)] * 8, 8), :] = w
                if k == 0:
                    bound_ref[pl.ds(NP + NH + UPP_AT[(i, j)], NQ, stride=BOTH), :] = w
            old_h = None if last else {m: h_ref[pl.ds((m * NV + j) * 8, 8), :] for m in range(NV)}
            for i in range(NV):
                terms = [] if last else [upp[(i, m)] * old_h[m] for m in range(i, NV)]
                if i >= j:
                    terms.append(g_ref[g_at(k, i, j), :])
                h = total(terms) if terms else jnp.zeros((8, 128), F32)
                h_ref[pl.ds((i * NV + j) * 8, 8), :] = h
                if k == 0:
                    bound_ref[pl.ds(NP + i * NV + j, NQ, stride=BOTH), :] = h

    return [partial(forward_step, k) for k in range(KN)] + [partial(backward_step, k) for k in range(KN - 1, -1, -1)]


def residual_kernel(
    with_products,
    me_ref,
    recv_ref,
    recv_cells_ref,
    face_weight_ref,
    iface_cells_ref,
    donor_ref,
    iface_weight_ref,
    cells_ref,
    source_ref,
    low_ref,
    upp_ref,
    jac_ref,
    inv_ref,
    *refs,
):
    steps = []
    if with_products:
        bound_ref, drive_ref, lowc_ref, uppc_ref, acc_ref, x_ref, y_ref, r_ref, g_ref, h_ref, w_ref = refs
        steps = product_steps(low_ref, upp_ref, lowc_ref, uppc_ref, bound_ref, g_ref, h_ref, w_ref)
        low_ref, upp_ref = lowc_ref, uppc_ref
    else:
        bound_ref, drive_ref, acc_ref, x_ref, y_ref, r_ref = refs
    stride = BOTH if with_products else ENDS
    def add_slots(values, target):
        row = jnp.right_shift(target, 7)
        lane = jnp.bitwise_and(target, 127)
        hot_row = one_hot(jnp.bitwise_and(row, 63), 64)
        hot_lane = one_hot(jnp.right_shift(row, 6) * 128 + lane, 256)
        parts = []
        for v in range(NV):
            wide = jnp.broadcast_to(values[v], (16, values[v].shape[1]))
            parts.append(split_two(wide))
        left = jnp.concatenate(
            [hot_row * jnp.concatenate([parts[v][h]] * 4, axis=0) for h in range(2) for v in range(NV)], axis=0
        )
        acc_ref[...] += lax.dot_general(
            left, hot_lane, (((1,), (1,)), ((), ())), preferred_element_type=F32
        )

    def uncoupled(k):
        a = [cells_ref[pl.ds(v * 128 + k * 8, 8), :] for v in range(NV)]
        for i in range(NV):
            product = total(at_k(jac_ref, i * NV + j, k) * a[j] for j in range(NV))
            r_ref[pl.ds((i * KN + k) * 8, 8), :] = at_k(source_ref, i, k) - product

    acc_ref[...] = jnp.zeros_like(acc_ref)
    for n in range(NB - 1):
        p = other_block(me_ref, n)
        weight = face_weight_ref[pl.ds(p, 1), :]
        came = recv_ref[pl.ds(pl.multiple_of(p * 48, 8), 48), :]
        values = []
        for v in range(NV):
            rows = [c * 12 + v for c in range(4)]
            values.append(jnp.concatenate([came[r : r + 1] for r in rows], axis=1) * weight)
        add_slots(values, recv_cells_ref[pl.ds(p, 1), :])
        uncoupled(n)
        for step in steps[3 * n : 3 * n + 3]:
            step()
    uncoupled(KN - 1)

    for v in range(NV):
        stage_table(recv_ref[pl.ds(6 + v, 64, stride=12), :], x_ref, v, 64)
    first = pick(x_ref, donor_ref[0:1, :], 64)
    second = pick(x_ref, donor_ref[1:2, :], 64)
    w0 = iface_weight_ref[0:1, :]
    w1 = iface_weight_ref[1:2, :]
    add_slots([first[v] * w0 + second[v] * w1 for v in range(NV)], iface_cells_ref[...])

    y = None
    for k in range(KN):
        r = []
        half, row = k // 8, (k % 8) * 8
        lanes = slice(half * 128, half * 128 + 128)
        for i in range(NV):
            coupled = acc_ref[i * 64 + row : i * 64 + row + 8, lanes]
            coupled = coupled + acc_ref[384 + i * 64 + row : 384 + i * 64 + row + 8, lanes]
            r.append(r_ref[pl.ds((i * KN + k) * 8, 8), :] + coupled)
        d = [total(at_k(inv_ref, i * NV + j, k) * r[j] for j in range(NV)) for i in range(NV)]
        if k == 0:
            y = d
        else:
            y = [d[i] + total(low_ref[pl.ds((LOW_AT[(i, j)] * KN + k) * 8, 8), :] * y[j] for j in range(i + 1)) for i in range(NV)]
        for i in range(NV):
            drive_ref[pl.ds(i * 128 + k * 8, 8), :] = d[i]
            y_ref[pl.ds(i * 128 + k * 8, 8), :] = y[i]
    u = y
    for k in range(KN - 2, -1, -1):
        u = [
            y_ref[pl.ds(i * 128 + k * 8, 8), :]
            + total(upp_ref[pl.ds((UPP_AT[(i, j)] * KN + k) * 8, 8), :] * u[j] for j in range(i, NV))
            for i in range(NV)
        ]
    for i in range(NV):
        bound_ref[pl.ds(stride - ENDS + i, NQ, stride=stride), :] = y[i]
        bound_ref[pl.ds(stride - ENDS + NV + i, NQ, stride=stride), :] = u[i]


def boundary_kernel(stride, phw_ref, *refs):
    *bounds, out_ref = refs
    bound_ref = bounds[0] if bounds else phw_ref

    def end_at(p, n):
        at = (p + 1) * stride - ENDS + n
        return bound_ref[at : at + 1, :]

    def factor(p, n):
        return phw_ref[p * BOTH + n : p * BOTH + n + 1, :]

    zero = jnp.zeros((1, 128), F32)
    y = [zero] * NV
    entering = []
    for p in range(NQ):
        entering.append(y)
        for i in range(NV):
            out_ref[p * ENDS + i : p * ENDS + i + 1, :] = y[i]
        if p + 1 < NQ:
            y = [
                end_at(p, i)
                + total(factor(p, LOW_AT[(i, j)]) * y[j] for j in range(i + 1))
                for i in range(NV)
            ]
    u = [zero] * NV
    for p in range(NQ - 1, -1, -1):
        for i in range(NV):
            out_ref[p * ENDS + NV + i : p * ENDS + NV + i + 1, :] = u[i]
        if p > 0:
            y = entering[p]
            known = [
                end_at(p, NV + i) + total(factor(p, NP + i * NV + j) * y[j] for j in range(NV))
                for i in range(NV)
            ]
            u = [
                known[i] + total(factor(p, NP + NH + UPP_AT[(i, j)]) * u[j] for j in range(i, NV))
                for i in range(NV)
            ]


def solve_lines(enter_ref, drive_ref, low_ref, upp_ref, cells_ref, y_ref, put):
    y = [enter_ref[pl.ds(i, NQ, stride=ENDS), :] for i in range(NV)]
    u = [enter_ref[pl.ds(NV + i, NQ, stride=ENDS), :] for i in range(NV)]
    for k in range(KN):
        y = [
            drive_ref[pl.ds(i * 128 + k * 8, 8), :]
            + total(low_ref[pl.ds((LOW_AT[(i, j)] * KN + k) * 8, 8), :] * y[j] for j in range(i + 1))
            for i in range(NV)
        ]
        for i in range(NV):
            y_ref[pl.ds(i * 128 + k * 8, 8), :] = y[i]
    for k in range(KN - 1, -1, -1):
        u = [
            y_ref[pl.ds(i * 128 + k * 8, 8), :]
            + total(upp_ref[pl.ds((UPP_AT[(i, j)] * KN + k) * 8, 8), :] * u[j] for j in range(i, NV))
            for i in range(NV)
        ]
        for i in range(NV):
            put(i, k, cells_ref[pl.ds(i * 128 + k * 8, 8), :] + u[i])


def update_kernel(me_ref, enter_ref, drive_ref, low_ref, upp_ref, cells_ref, picks_ref, out_ref, new_ref, y_ref, x_ref):
    def put(i, k, value):
        new_ref[pl.ds(i * 128 + k * 8, 8), :] = value

    solve_lines(enter_ref, drive_ref, low_ref, upp_ref, cells_ref, y_ref, put)
    gather_all(me_ref, new_ref, picks_ref, out_ref, x_ref)


def final_kernel(enter_ref, drive_ref, low_ref, upp_ref, cells_ref, new_ref, y_ref):
    def put(i, k, value):
        put_k(new_ref, i, k, value)

    solve_lines(enter_ref, drive_ref, low_ref, upp_ref, cells_ref, y_ref, put)


def f32(*shape):
    return jax.ShapeDtypeStruct(shape, F32)


PARAMS = pltpu.CompilerParams(vmem_limit_bytes=20 * 1024 * 1024)


def body(
    adjoint_start, source, jacobian, inv_diag, lower_prop, upper_prop, send_cells, recv_cells,
    face_weight, cycle_cells, iface_cells, iface_donor, iface_weight,
):
    start = rows_of(adjoint_start)
    src = rows_of(source)
    jac = rows_of(jacobian)
    inv = rows_of(inv_diag)
    low = rows_of(lower_prop)
    upp = rows_of(upper_prop)
    send = send_cells.reshape(NB, 512)
    recv_at = recv_cells.reshape(NB, 512)
    weight = face_weight.reshape(NB, 512)
    picks = jnp.concatenate([send, cycle_cells.reshape(1, 512)], axis=0)
    iface_at = iface_cells.reshape(1, 512)
    donor = iface_donor.reshape(2, 512)
    iface_w = iface_weight.reshape(2, 512)

    me = lax.axis_index("block").reshape(1).astype(jnp.int32)

    def call(kernel, name, out, operands, scratch=(), flops=0):
        size = sum(4 * x.size for x in operands)
        return pl.pallas_call(
            kernel,
            out_shape=out,
            in_specs=[SMEM if x is me else VMEM for x in operands],
            out_specs=jax.tree.map(lambda _: VMEM, out),
            scratch_shapes=list(scratch),
            compiler_params=PARAMS,
            cost_estimate=pl.CostEstimate(flops=flops, bytes_accessed=size, transcendentals=0),
            name=name,
        )(*operands)

    def exchange(x, axis, parts):
        x = x.reshape(parts, x.size // (parts * 128), 128)
        return lax.all_to_all(x, axis, split_axis=0, concat_axis=0, tiled=True)

    field = f32(NV * 128, 128)
    faces = f32(NB, 48, 128)
    table = pltpu.VMEM((768, 256), BF16)
    lines = pltpu.VMEM((NV * 128, 128), F32)
    outgoing, cells = call(first_gather_kernel, "first_gather", (faces, field), (me, start, picks), [table], FIRST_HINT * PICK)
    lowc, uppc = low, upp
    for iteration in range(ITERS):
        incoming = exchange(outgoing, "block", NB)
        operands = (recv_at, weight, iface_at, donor, iface_w, cells, src)
        stride = ENDS
        operands = (me, incoming.reshape(NB * 48, 128)) + operands + (lowc, uppc, jac, inv)
        scratch = [pltpu.VMEM((768, 256), F32), pltpu.VMEM((768, 128), BF16), lines, lines]
        if iteration == 0:
            stride = BOTH
            compact = f32(NP * 128, 128)
            more = [pltpu.VMEM((KN * NP * 8, 128), F32), pltpu.VMEM((NH * 8, 128), F32), pltpu.VMEM((NP * 8, 128), F32)]
            bound, drive, lowc, uppc = call(
                partial(residual_kernel, True),
                "residual",
                (f32(NQ * stride, 128), field, compact, compact),
                operands,
                scratch + more,
                PICK,
            )
        else:
            bound, drive = call(
                partial(residual_kernel, False), "residual", (f32(NQ * stride, 128), field), operands, scratch, PICK
            )
        bound = exchange(bound, "line", NQ).reshape(NQ * stride, 128)
        if iteration == 0:
            products = bound
            operands = (bound,)
        else:
            operands = (products, bound)
        enter = call(partial(boundary_kernel, stride), "boundary", f32(NQ * ENDS, 128), operands)
        enter = exchange(enter, "line", NQ).reshape(NQ * ENDS, 128)
        operands = (enter, drive, lowc, uppc, cells)
        if iteration + 1 < ITERS:
            outgoing, cells = call(update_kernel, "update", (faces, field), (me,) + operands + (picks,), [lines, table], PICK)
        else:
            result = call(final_kernel, "final_update", field, operands, [lines])
    return from_rows(result, NV)[:, None]


def solution(mesh):
    cell = P(None, "block", "line", None)
    matrix = P(None, None, "block", "line", None)
    slots = P("block", "line", None, None)
    flat = P("block", "line", None)
    placed = (cell, cell, matrix, matrix, matrix, matrix, slots, slots, slots, flat, flat, slots, slots)
    return jax.shard_map(body, mesh=mesh, in_specs=placed, out_specs=cell, check_vma=False)
```

```python
from functools import partial

import jax
import jax.numpy as jnp
from jax import lax
from jax.experimental import pallas as pl
from jax.experimental.pallas import tpu as pltpu
from jax.sharding import PartitionSpec as P

NV = 6
KN = 16
NB = 16
NQ = 8
ITERS = 2
FIRST_HINT = 6
PICK = 2 * 768 * 256 * 17 * 512
F32 = jnp.float32
BF16 = jnp.bfloat16
LOW = [(i, j) for i in range(NV) for j in range(i + 1)]
UPP = [(i, j) for i in range(NV) for j in range(i, NV)]
LOW_AT = {ij: n for n, ij in enumerate(LOW)}
UPP_AT = {ij: n for n, ij in enumerate(UPP)}
NP = len(LOW)
NH = NV * NV
NPHW = 2 * NP + NH
ROWS = 80
ENDS = 16
BOTH = ROWS + ENDS

VMEM = pl.BlockSpec(memory_space=pltpu.VMEM)
HBM = pl.BlockSpec(memory_space=pltpu.HBM)
SMEM = pl.BlockSpec(memory_space=pltpu.SMEM)


def rows_of(x):
    n = x.size // (16 * 1024)
    x = x.reshape(n, 2, 8, 8, 128)
    return jnp.transpose(x, (0, 1, 3, 2, 4)).reshape(n * 128, 128)


def from_rows(x, n):
    x = x.reshape(n, 2, 8, 8, 128)
    return jnp.transpose(x, (0, 1, 3, 2, 4)).reshape(n, 16, 1024)


def at_k(ref, n, k):
    return ref[pl.ds(n * 128 + (k // 8) * 64 + k % 8, 8, stride=8), :]


def put_k(ref, n, k, value):
    ref[pl.ds(n * 128 + (k // 8) * 64 + k % 8, 8, stride=8), :] = value


def total(terms):
    terms = list(terms)
    while len(terms) > 1:
        nxt = [terms[i] + terms[i + 1] for i in range(0, len(terms) - 1, 2)]
        if len(terms) % 2:
            nxt.append(terms[-1])
        terms = nxt
    return terms[0]


def split_two(x):
    high = x.astype(BF16)
    low = (x - high.astype(F32)).astype(BF16)
    return high, low


def one_hot(index, count):
    rows = lax.broadcasted_iota(jnp.int32, (count, index.shape[1]), 0)
    return jnp.where(rows == index, 1.0, 0.0).astype(BF16)


def stage_table(table, x_ref, v, rows):
    t = table.T
    t = jnp.concatenate([t[:64], t[64:]], axis=1)
    high, low = split_two(t)
    x_ref[v * 64 : v * 64 + 64, 0 : 2 * rows] = high
    x_ref[384 + v * 64 : 384 + v * 64 + 64, 0 : 2 * rows] = low


def pick(x_ref, cell, rows):
    lane = jnp.bitwise_and(cell, 127)
    row = jnp.right_shift(cell, 7)
    key = jnp.right_shift(lane, 6) * rows + row
    low = jnp.bitwise_and(lane, 63)
    t = jnp.dot(x_ref[:, : 2 * rows], one_hot(key, 2 * rows), preferred_element_type=F32)
    t = t[:384] + t[384:]
    mask = lax.broadcasted_iota(jnp.int32, (64, cell.shape[1]), 0) == low
    return [
        jnp.sum(jnp.where(mask, t[v * 64 : (v + 1) * 64], 0.0), axis=0, keepdims=True) for v in range(NV)
    ]


def other_block(me_ref, n):
    return jnp.bitwise_and(me_ref[0] + 1 + n, NB - 1)


def gather_all(me_ref, cells_ref, picks_ref, out_ref, x_ref):
    for v in range(NV):
        stage_table(cells_ref[pl.ds(v * 128, 128), :], x_ref, v, 128)
    for n in range(NB - 1):
        p = other_block(me_ref, n)
        got = pick(x_ref, jnp.maximum(picks_ref[pl.ds(p, 1), :], 0), 128)
        for v in range(NV):
            for c in range(4):
                out_ref[p, c * 12 + v : c * 12 + v + 1, :] = got[v][:, c * 128 : (c + 1) * 128]
    got = pick(x_ref, picks_ref[NB : NB + 1, :], 128)
    for v in range(NV):
        for c in range(4):
            r = c * 12 + 6 + v
            piece = jnp.broadcast_to(got[v][:, c * 128 : (c + 1) * 128][None], (NB, 1, 128))
            out_ref[:, r : r + 1, :] = piece


def first_gather_kernel(me_ref, start_ref, picks_ref, out_ref, cells_ref, x_ref):
    for v in range(NV):
        for k in range(KN):
            cells_ref[pl.ds((v * KN + k) * 8, 8), :] = at_k(start_ref, v, k)
    gather_all(me_ref, cells_ref, picks_ref, out_ref, x_ref)


def product_steps(low_ref, upp_ref, lowc_ref, uppc_ref, bound_ref, g_ref, h_ref, w_ref):
    def g_at(k, i, j):
        return pl.ds((k * NP + LOW_AT[(i, j)]) * 8, 8)

    def forward_step(k):
        low = {(i, j): at_k(low_ref, i * NV + j, k) for (i, j) in LOW}
        for i, j in LOW:
            lowc_ref[pl.ds((LOW_AT[(i, j)] * KN + k) * 8, 8), :] = low[(i, j)]
        for j in range(NV):
            before = {m: g_ref[g_at(k - 1, m, j), :] for m in range(j, NV)} if k else None
            for i in range(j, NV):
                g = total(low[(i, m)] * before[m] for m in range(j, i + 1)) if k else low[(i, j)]
                g_ref[g_at(k, i, j), :] = g
                if k == KN - 1:
                    bound_ref[pl.ds(LOW_AT[(i, j)], NQ, stride=BOTH), :] = g

    def backward_step(k):
        upp = {(i, j): at_k(upp_ref, i * NV + j, k) for (i, j) in UPP}
        for i, j in UPP:
            uppc_ref[pl.ds((UPP_AT[(i, j)] * KN + k) * 8, 8), :] = upp[(i, j)]
        last = k == KN - 1
        for j in range(NV):
            old_w = None if last else {m: w_ref[pl.ds(UPP_AT[(m, j)] * 8, 8), :] for m in range(j + 1)}
            for i in range(j + 1):
                w = upp[(i, j)] if last else total(upp[(i, m)] * old_w[m] for m in range(i, j + 1))
                w_ref[pl.ds(UPP_AT[(i, j)] * 8, 8), :] = w
                if k == 0:
                    bound_ref[pl.ds(NP + NH + UPP_AT[(i, j)], NQ, stride=BOTH), :] = w
            old_h = None if last else {m: h_ref[pl.ds((m * NV + j) * 8, 8), :] for m in range(NV)}
            for i in range(NV):
                terms = [] if last else [upp[(i, m)] * old_h[m] for m in range(i, NV)]
                if i >= j:
                    terms.append(g_ref[g_at(k, i, j), :])
                h = total(terms) if terms else jnp.zeros((8, 128), F32)
                h_ref[pl.ds((i * NV + j) * 8, 8), :] = h
                if k == 0:
                    bound_ref[pl.ds(NP + i * NV + j, NQ, stride=BOTH), :] = h

    return [partial(forward_step, k) for k in range(KN)] + [partial(backward_step, k) for k in range(KN - 1, -1, -1)]


def residual_kernel(
    with_products,
    me_ref,
    recv_ref,
    recv_cells_ref,
    face_weight_ref,
    iface_cells_ref,
    donor_ref,
    iface_weight_ref,
    cells_ref,
    source_ref,
    low_ref,
    upp_ref,
    jac_ref,
    inv_ref,
    *refs,
):
    steps = []
    if with_products:
        bound_ref, drive_ref, lowc_ref, uppc_ref, acc_ref, x_ref, y_ref, r_ref, g_ref, h_ref, w_ref = refs
        steps = product_steps(low_ref, upp_ref, lowc_ref, uppc_ref, bound_ref, g_ref, h_ref, w_ref)
        low_ref, upp_ref = lowc_ref, uppc_ref
    else:
        bound_ref, drive_ref, acc_ref, x_ref, y_ref, r_ref = refs
    stride = BOTH if with_products else ENDS
    def add_slots(values, target, begins=False):
        row = jnp.right_shift(target, 7)
        lane = jnp.bitwise_and(target, 127)
        hot_row = one_hot(jnp.bitwise_and(row, 63), 64)
        hot_lane = one_hot(jnp.right_shift(row, 6) * 128 + lane, 256)
        parts = []
        for v in range(NV):
            wide = jnp.broadcast_to(values[v], (16, values[v].shape[1]))
            parts.append(split_two(wide))
        left = jnp.concatenate(
            [hot_row * jnp.concatenate([parts[v][h]] * 4, axis=0) for h in range(2) for v in range(NV)], axis=0
        )
        product = lax.dot_general(left, hot_lane, (((1,), (1,)), ((), ())), preferred_element_type=F32)
        acc_ref[...] = product if begins else acc_ref[...] + product

    def uncoupled(k):
        a = [cells_ref[pl.ds(v * 128 + k * 8, 8), :] for v in range(NV)]
        for i in range(NV):
            product = total(at_k(jac_ref, i * NV + j, k) * a[j] for j in range(NV))
            r_ref[pl.ds((i * KN + k) * 8, 8), :] = at_k(source_ref, i, k) - product

    for n in range(NB - 1):
        p = other_block(me_ref, n)
        weight = face_weight_ref[pl.ds(p, 1), :]
        came = recv_ref[pl.ds(pl.multiple_of(p * 48, 8), 48), :]
        values = []
        for v in range(NV):
            rows = [c * 12 + v for c in range(4)]
            values.append(jnp.concatenate([came[r : r + 1] for r in rows], axis=1) * weight)
        add_slots(values, recv_cells_ref[pl.ds(p, 1), :], n == 0)
        uncoupled(n)
        for step in steps[len(steps) * n // (NB - 1) : len(steps) * (n + 1) // (NB - 1)]:
            step()
    uncoupled(KN - 1)

    for v in range(NV):
        stage_table(recv_ref[pl.ds(6 + v, 64, stride=12), :], x_ref, v, 64)
    first = pick(x_ref, donor_ref[0:1, :], 64)
    second = pick(x_ref, donor_ref[1:2, :], 64)
    w0 = iface_weight_ref[0:1, :]
    w1 = iface_weight_ref[1:2, :]
    add_slots([first[v] * w0 + second[v] * w1 for v in range(NV)], iface_cells_ref[...])

    y = None
    for k in range(KN):
        r = []
        half, row = k // 8, (k % 8) * 8
        lanes = slice(half * 128, half * 128 + 128)
        for i in range(NV):
            coupled = acc_ref[i * 64 + row : i * 64 + row + 8, lanes]
            coupled = coupled + acc_ref[384 + i * 64 + row : 384 + i * 64 + row + 8, lanes]
            r.append(r_ref[pl.ds((i * KN + k) * 8, 8), :] + coupled)
        d = [total(at_k(inv_ref, i * NV + j, k) * r[j] for j in range(NV)) for i in range(NV)]
        if k == 0:
            y = d
        else:
            y = [d[i] + total(low_ref[pl.ds((LOW_AT[(i, j)] * KN + k) * 8, 8), :] * y[j] for j in range(i + 1)) for i in range(NV)]
        for i in range(NV):
            drive_ref[pl.ds(i * 128 + k * 8, 8), :] = d[i]
            y_ref[pl.ds(i * 128 + k * 8, 8), :] = y[i]
    u = y
    for k in range(KN - 2, -1, -1):
        u = [
            y_ref[pl.ds(i * 128 + k * 8, 8), :]
            + total(upp_ref[pl.ds((UPP_AT[(i, j)] * KN + k) * 8, 8), :] * u[j] for j in range(i, NV))
            for i in range(NV)
        ]
    for i in range(NV):
        bound_ref[pl.ds(stride - ENDS + i, NQ, stride=stride), :] = y[i]
        bound_ref[pl.ds(stride - ENDS + NV + i, NQ, stride=stride), :] = u[i]


def boundary_kernel(stride, phw_ref, *refs):
    *bounds, out_ref = refs
    bound_ref = bounds[0] if bounds else phw_ref

    def end_at(p, n):
        at = (p + 1) * stride - ENDS + n
        return bound_ref[at : at + 1, :]

    def factor(p, n):
        return phw_ref[p * BOTH + n : p * BOTH + n + 1, :]

    zero = jnp.zeros((1, 128), F32)
    y = [zero] * NV
    entering = []
    for p in range(NQ):
        entering.append(y)
        for i in range(NV):
            out_ref[p * ENDS + i : p * ENDS + i + 1, :] = y[i]
        if p + 1 < NQ:
            y = [
                end_at(p, i)
                + total(factor(p, LOW_AT[(i, j)]) * y[j] for j in range(i + 1))
                for i in range(NV)
            ]
    u = [zero] * NV
    for p in range(NQ - 1, -1, -1):
        for i in range(NV):
            out_ref[p * ENDS + NV + i : p * ENDS + NV + i + 1, :] = u[i]
        if p > 0:
            y = entering[p]
            known = [
                end_at(p, NV + i) + total(factor(p, NP + i * NV + j) * y[j] for j in range(NV))
                for i in range(NV)
            ]
            u = [
                known[i] + total(factor(p, NP + NH + UPP_AT[(i, j)]) * u[j] for j in range(i, NV))
                for i in range(NV)
            ]


def solve_lines(enter_ref, drive_ref, low_ref, upp_ref, cells_ref, y_ref, put):
    y = [enter_ref[pl.ds(i, NQ, stride=ENDS), :] for i in range(NV)]
    u = [enter_ref[pl.ds(NV + i, NQ, stride=ENDS), :] for i in range(NV)]
    for k in range(KN):
        y = [
            drive_ref[pl.ds(i * 128 + k * 8, 8), :]
            + total(low_ref[pl.ds((LOW_AT[(i, j)] * KN + k) * 8, 8), :] * y[j] for j in range(i + 1))
            for i in range(NV)
        ]
        for i in range(NV):
            y_ref[pl.ds(i * 128 + k * 8, 8), :] = y[i]
    for k in range(KN - 1, -1, -1):
        u = [
            y_ref[pl.ds(i * 128 + k * 8, 8), :]
            + total(upp_ref[pl.ds((UPP_AT[(i, j)] * KN + k) * 8, 8), :] * u[j] for j in range(i, NV))
            for i in range(NV)
        ]
        for i in range(NV):
            put(i, k, cells_ref[pl.ds(i * 128 + k * 8, 8), :] + u[i])


def update_kernel(me_ref, enter_ref, drive_ref, low_ref, upp_ref, cells_ref, picks_ref, out_ref, new_ref, y_ref, x_ref):
    def put(i, k, value):
        new_ref[pl.ds(i * 128 + k * 8, 8), :] = value

    solve_lines(enter_ref, drive_ref, low_ref, upp_ref, cells_ref, y_ref, put)
    gather_all(me_ref, new_ref, picks_ref, out_ref, x_ref)


def final_kernel(enter_ref, drive_ref, low_ref, upp_ref, cells_ref, new_ref, y_ref):
    def put(i, k, value):
        put_k(new_ref, i, k, value)

    solve_lines(enter_ref, drive_ref, low_ref, upp_ref, cells_ref, y_ref, put)


def f32(*shape):
    return jax.ShapeDtypeStruct(shape, F32)


PARAMS = pltpu.CompilerParams(vmem_limit_bytes=20 * 1024 * 1024)


def body(
    adjoint_start, source, jacobian, inv_diag, lower_prop, upper_prop, send_cells, recv_cells,
    face_weight, cycle_cells, iface_cells, iface_donor, iface_weight,
):
    start = rows_of(adjoint_start)
    src = rows_of(source)
    jac = rows_of(jacobian)
    inv = rows_of(inv_diag)
    low = rows_of(lower_prop)
    upp = rows_of(upper_prop)
    send = send_cells.reshape(NB, 512)
    recv_at = recv_cells.reshape(NB, 512)
    weight = face_weight.reshape(NB, 512)
    picks = jnp.concatenate([send, cycle_cells.reshape(1, 512)], axis=0)
    iface_at = iface_cells.reshape(1, 512)
    donor = iface_donor.reshape(2, 512)
    iface_w = iface_weight.reshape(2, 512)

    me = lax.axis_index("block").reshape(1).astype(jnp.int32)

    def call(kernel, name, out, operands, scratch=(), flops=0):
        size = sum(4 * x.size for x in operands)
        return pl.pallas_call(
            kernel,
            out_shape=out,
            in_specs=[SMEM if x is me else VMEM for x in operands],
            out_specs=jax.tree.map(lambda _: VMEM, out),
            scratch_shapes=list(scratch),
            compiler_params=PARAMS,
            cost_estimate=pl.CostEstimate(flops=flops, bytes_accessed=size, transcendentals=0),
            name=name,
        )(*operands)

    def exchange(x, axis, parts):
        x = x.reshape(parts, x.size // (parts * 128), 128)
        return lax.all_to_all(x, axis, split_axis=0, concat_axis=0, tiled=True)

    field = f32(NV * 128, 128)
    faces = f32(NB, 48, 128)
    table = pltpu.VMEM((768, 256), BF16)
    lines = pltpu.VMEM((NV * 128, 128), F32)
    outgoing, cells = call(first_gather_kernel, "first_gather", (faces, field), (me, start, picks), [table], FIRST_HINT * PICK)
    lowc, uppc = low, upp
    for iteration in range(ITERS):
        incoming = exchange(outgoing, "block", NB)
        operands = (recv_at, weight, iface_at, donor, iface_w, cells, src)
        stride = ENDS
        operands = (me, incoming.reshape(NB * 48, 128)) + operands + (lowc, uppc, jac, inv)
        scratch = [pltpu.VMEM((768, 256), F32), pltpu.VMEM((768, 128), BF16), lines, lines]
        if iteration == 0:
            stride = BOTH
            compact = f32(NP * 128, 128)
            more = [pltpu.VMEM((KN * NP * 8, 128), F32), pltpu.VMEM((NH * 8, 128), F32), pltpu.VMEM((NP * 8, 128), F32)]
            bound, drive, lowc, uppc = call(
                partial(residual_kernel, True),
                "residual",
                (f32(NQ * stride, 128), field, compact, compact),
                operands,
                scratch + more,
                PICK,
            )
        else:
            bound, drive = call(
                partial(residual_kernel, False), "residual", (f32(NQ * stride, 128), field), operands, scratch, PICK
            )
        bound = exchange(bound, "line", NQ).reshape(NQ * stride, 128)
        if iteration == 0:
            products = bound
            operands = (bound,)
        else:
            operands = (products, bound)
        enter = call(partial(boundary_kernel, stride), "boundary", f32(NQ * ENDS, 128), operands)
        enter = exchange(enter, "line", NQ).reshape(NQ * ENDS, 128)
        operands = (enter, drive, lowc, uppc, cells)
        if iteration + 1 < ITERS:
            outgoing, cells = call(update_kernel, "update", (faces, field), (me,) + operands + (picks,), [lines, table], PICK)
        else:
            result = call(final_kernel, "final_update", field, operands, [lines])
    return from_rows(result, NV)[:, None]


def solution(mesh):
    cell = P(None, "block", "line", None)
    matrix = P(None, None, "block", "line", None)
    slots = P("block", "line", None, None)
    flat = P("block", "line", None)
    placed = (cell, cell, matrix, matrix, matrix, matrix, slots, slots, slots, flat, flat, slots, slots)
    return jax.shard_map(body, mesh=mesh, in_specs=placed, out_specs=cell, check_vma=False)
```
